32 devices in a mesh: groups: 2 (over x), side: 2 (over core), attn: 8 (over z, y).
Axes of the slice: x: 2, y: 2, z: 4, core: 2. Of those that a mesh axis runs over, the one named last changes fastest.
Arguments:
- hidden_in: bfloat16 [128, 6144], P(('groups', 'side', 'attn')), parts along dimension 0, may hold values from -24 to 24
- norm_gain: bfloat16 [6144], replicated, may hold values from 0.25 to 1.75
- routes: int32 [128, 2], P(('groups', 'side', 'attn')), parts along dimension 0, may hold values from 0 to 3, all different within a row; in each aligned block of 4 rows (0 to 3, 4 to 7, ...) at most 3 rows name the same one
- route_gates: bfloat16 [128, 2], P(('groups', 'side', 'attn')), parts along dimension 0, may hold values from 0.099609375 to 0.8984375
- w_gate: bfloat16 [6144, 40960], P(None, ('side', 'attn')), may hold values from -0.078125 to 0.078125
- w_up: bfloat16 [6144, 40960], P(None, ('side', 'attn')), may hold values from -0.078125 to 0.078125
- w_down: bfloat16 [40960, 6144], P(('side', 'attn')), may hold values from -0.0625 to 0.0625
Outputs:
- mixed: bfloat16 [128, 6144], P(('groups', 'side', 'attn')), parts along dimension 0
The draws below stay inside these ranges and needn't reach their ends.
There are 2 independent parts, one for each index of `groups`. The reference program is written for one: setup_inputs(seed, part) draws one part's arguments, and reference() takes and returns one part's arrays. A program takes and returns all parts, laid end to end along the dimension named above; an argument that names none is the same for every part. Nothing has to cross between parts.
Inputs may be any that keep to these rules, and one draw needn't show every extreme that they name: `routes`: each session names 2 different experts; no expert is named by more than 3 of the rows of one device.
All inputs are finite; a program needn't handle non-finite values.
Results may differ from the reference program's by a relative error of at most 0.0065.
Values may be sent and summed in bfloat16 or wider, within the bound.
No kernel may reach another device: no remote copies, remote signals or barrier semaphores. Data moves between devices by JAX's collectives and lax.ppermute only.
A program may use at most 192 MiB of HBM per device.

```python
import math
import jax
import jax.numpy as jnp
import numpy as np
from jax import lax

D = 6144
FF = 10240
EXPERTS = 4
TOP = 2
SESS_DEV = 4
CAP = 3
SESSIONS = 64


def draw_hidden_in(key, part):
    key = jax.random.fold_in(key, 17)
    key_rows, key_cols, key_base = jax.random.split(key, 3)
    row_scale = jnp.exp(jax.random.uniform(key_rows, (SESSIONS, 1), jnp.float32, math.log(0.5), math.log(2.0)))
    base = jnp.clip(jax.random.normal(key_base, (SESSIONS, D), jnp.float32), -4.0, 4.0)
    col_scale = jnp.exp(jax.random.uniform(key_cols, (1, D), jnp.float32, math.log(0.3), math.log(3.0)))
    return (base * row_scale * col_scale).astype(jnp.bfloat16)


def steps_of(own_key, shape, cuts, low, high):
    factor_of = 1.0
    for dim, blocks in cuts:
        draws = jax.random.uniform(jax.random.fold_in(jax.random.fold_in(own_key, 6), dim), (blocks,), jnp.float32, low / len(cuts), high / len(cuts))
        factor_of = factor_of * jnp.repeat(jnp.exp(draws), shape[dim] // blocks).reshape((-1,) + (1,) * (len(shape) - 1 - dim))
    return factor_of


def assign_block(key, own, number, rows, count, top, bound, skew):
    sequence = jax.random.permutation(key, count)
    crowded, usual = load_shares(count, rows * top, bound, skew, True), load_shares(count, rows * top, bound, skew, False)
    places = jnp.arange(count)

    def named(lengths, rotation):
        used = int((lengths > 0).sum())
        fixed = max(1, used // 4)
        shifted = fixed + (places - fixed + rotation * (used - fixed)) % max(1, count - fixed)
        return jnp.zeros((count,), jnp.int32).at[sequence[jnp.where(places < fixed, places, shifted)]].set(jnp.asarray(lengths, jnp.int32))

    lengths = jnp.where(number % 4 == 0, named(crowded, number // 4), named(usual, number - number // 4 - 1))
    mixed = jax.random.permutation(jax.random.fold_in(own, 3), count)
    giver, sink = mixed[0:count // 2 * 2:2], mixed[1:count // 2 * 2:2]
    slack = jnp.minimum(lengths[giver] - 1, bound - lengths[sink]) // 2
    slack = jnp.where((giver == sequence[0]) | (sink == sequence[0]) | (lengths[sink] == 0), 0, jnp.maximum(slack, 0))
    shifted = jax.random.randint(jax.random.fold_in(own, 4), (count // 2,), 0, 1 << 20) % (slack + 1)
    lengths = lengths.at[giver].add(-shifted).at[sink].add(shifted)
    members = jnp.searchsorted(jnp.cumsum(lengths), jnp.arange(rows * top), side="right").astype(jnp.int32)
    grid = members.reshape(top, rows).T
    grid = grid[jax.random.permutation(jax.random.fold_in(own, 1), rows)]
    rotation = jax.random.randint(jax.random.fold_in(own, 2), (rows, 1), 0, top)
    return jnp.take_along_axis(grid, (jnp.arange(top)[None, :] + rotation) % top, axis=1)


def load_shares(amount, total, limit, lean, full):
    portions = [(1 << 20) // math.isqrt(rank ** lean) + 1 for rank in range(1, amount + 1)]
    largest = limit if full else min(limit, max(-(-total // amount), total * portions[0] // sum(portions)))
    least = 1 if total - largest >= amount - 1 else 0
    holding, surplus = [largest] + [least] * (amount - 1), total - largest - least * (amount - 1)
    while surplus > 0:
        movable = [i for i in range(1, amount) if holding[i] < largest] or [i for i in range(1, amount) if holding[i] < limit]
        whole, budget = sum([portions[i] for i in movable]), surplus
        for i in movable:
            extra = min(limit - holding[i], max(1, budget * portions[i] // whole), surplus)
            holding[i] = holding[i] + extra
            surplus = surplus - extra
    return np.array(holding)


def scatter_about(stream_key, shape, deviation, limit, cuts=(), kind=jnp.bfloat16):
    factor_of = steps_of(stream_key, shape, cuts, -0.22, 0.18) if cuts else 1.0
    drawn = jax.random.normal(stream_key, shape, jnp.float32) * deviation * factor_of
    return jnp.minimum(jnp.maximum(drawn, -limit), limit).astype(kind)


def setup_inputs(seed: int = 0, part: int = 0) -> dict:
    key_list = jax.random.split(jax.random.key(seed), 8)
    part_keys = jax.random.split(jax.random.fold_in(key_list[7], part), 8)
    hidden_in = draw_hidden_in(jax.random.fold_in(jax.random.fold_in(key_list[7], part), 71), part)
    norm_gain = jnp.clip(1.0 + 0.15 * jax.random.normal(key_list[1], (D,), jnp.float32), 0.25, 1.75).astype(jnp.bfloat16)
    routes_keys = jax.random.split(jax.random.fold_in(part_keys[2], 1), SESSIONS // SESS_DEV)
    routes_turns = jax.random.permutation(jax.random.fold_in(part_keys[2], 3), SESSIONS // SESS_DEV)
    routes = jax.vmap(lambda own, number: assign_block(jax.random.fold_in(part_keys[2], 2), own, number, SESS_DEV, EXPERTS, TOP, CAP, 2))(routes_keys, routes_turns).reshape((SESSIONS, TOP))
    route_gates = jnp.clip(0.099609375 + 0.7988281 * jax.random.uniform(part_keys[3], (SESSIONS, TOP), jnp.float32) ** steps_of(part_keys[3], (SESSIONS, TOP), ((0, 16),), -0.2, 0.2), 0.099609375, 0.8984375).astype(jnp.bfloat16)
    w_gate = scatter_about(key_list[4], (D, EXPERTS * FF), D ** -0.5, 0.078125, ((1, 16),))
    w_up = scatter_about(key_list[5], (D, EXPERTS * FF), D ** -0.5, 0.078125, ((1, 16),))
    w_down = scatter_about(key_list[6], (EXPERTS * FF, D), FF ** -0.5, 0.0625, ((0, 16),))
    return {"hidden_in": hidden_in, "norm_gain": norm_gain, "routes": routes, "route_gates": route_gates, "w_gate": w_gate, "w_up": w_up, "w_down": w_down}


epsilon = 1e-05

def reference(hidden_in, norm_gain, routes, route_gates, w_gate, w_up, w_down):
    values = hidden_in.astype(jnp.float32)
    inverse = lax.rsqrt(lax.optimization_barrier(jnp.mean(values * values, axis=-1, keepdims=True)) + epsilon)
    normed = (values * inverse * norm_gain.astype(jnp.float32)).astype(jnp.bfloat16)
    labels = jnp.arange(EXPERTS, dtype=jnp.int32)
    chosen = routes[:, :, None] == labels[None, None, :]
    coefficient = lax.optimization_barrier(jnp.sum(jnp.where(chosen, route_gates[:, :, None].astype(jnp.float32), 0.0), axis=1))
    combined = jnp.zeros((SESSIONS, D), jnp.float32)
    for expert_id in range(EXPERTS):
        first_col = expert_id * FF
        last_col = first_col + FF
        gate_act = jnp.dot(normed, w_gate[:, first_col:last_col], preferred_element_type=jnp.float32)
        up_act = jnp.dot(normed, w_up[:, first_col:last_col], preferred_element_type=jnp.float32)
        hidden = (jax.nn.silu(gate_act) * up_act).astype(jnp.bfloat16)
        out_rows = jnp.dot(hidden, w_down[first_col:last_col, :], preferred_element_type=jnp.float32)
        combined = combined + coefficient[:, expert_id:expert_id + 1] * out_rows
    return combined.astype(jnp.bfloat16)
```

```python
import jax
import jax.numpy as jnp
from jax import lax
from jax.sharding import PartitionSpec as P

EXPERTS = 4
EPSILON = 1e-05
LANES = 128


def swap_sides(values):
    sides = lax.axis_size("side")
    return lax.ppermute(values, "side", [(i, sides - 1 - i) for i in range(sides)])


def swap_chips(values, distance):
    chips = lax.axis_size("attn")
    return lax.ppermute(values, "attn", [(i, i ^ distance) for i in range(chips)])


def shards(hidden_in, norm_gain, routes, route_gates, w_gate, w_up, w_down):
    rows, width = hidden_in.shape
    chips = lax.axis_size("attn")
    devices = lax.axis_size(("side", "attn"))
    my_expert = lax.axis_index(("side", "attn")) // (devices // EXPERTS)
    values = hidden_in.astype(jnp.float32)
    inverse = lax.rsqrt(jnp.mean(values * values, axis=-1, keepdims=True) + EPSILON)
    normed = (values * inverse * norm_gain.astype(jnp.float32)).astype(jnp.bfloat16)
    labels = jnp.arange(LANES, dtype=jnp.int32)
    chosen = routes[:, :, None] == labels[None, None, :]
    coefficient = jnp.sum(
        jnp.where(chosen, route_gates[:, :, None], jnp.zeros((), jnp.bfloat16)), axis=1
    )
    payload = jnp.concatenate([normed, coefficient], axis=1)
    mine = jnp.concatenate([payload] + [swap_chips(payload, d) for d in range(1, chips)], axis=0)
    everything = jnp.concatenate([mine, swap_sides(mine)], axis=0)
    inputs = everything[:, :width]
    column = lax.dynamic_slice_in_dim(everything, width + my_expert, 1, 1).astype(jnp.float32)
    gate = jnp.dot(inputs, w_gate, preferred_element_type=jnp.float32)
    up = jnp.dot(inputs, w_up, preferred_element_type=jnp.float32)
    hidden = (jax.nn.silu(gate) * up).astype(jnp.bfloat16)
    out = jnp.dot(hidden, w_down, preferred_element_type=jnp.float32) * column
    half = rows * chips
    arrived = swap_sides(out[half:].astype(jnp.bfloat16))
    summed = (out[:half] + arrived.astype(jnp.float32)).astype(jnp.bfloat16)
    total = summed[:rows].astype(jnp.float32)
    for d in range(1, chips):
        block = swap_chips(summed[d * rows : (d + 1) * rows], d)
        total = total + block.astype(jnp.float32)
    return total.astype(jnp.bfloat16)


def solution(mesh):
    return jax.shard_map(
        shards,
        mesh=mesh,
        in_specs=(
            P(("groups", "side", "attn"), None),
            P(),
            P(("groups", "side", "attn"), None),
            P(("groups", "side", "attn"), None),
            P(None, ("side", "attn")),
            P(None, ("side", "attn")),
            P(("side", "attn"), None),
        ),
        out_specs=P(("groups", "side", "attn"), None),
        check_vma=False,
    )
```

```python
import functools

import jax
import jax.numpy as jnp
from jax import lax
from jax.experimental import pallas as pl
from jax.experimental.pallas import tpu as pltpu
from jax.sharding import PartitionSpec as P

EXPERTS = 4
EPSILON = 1e-05
LANES = 128
MIB = 1 << 20
MIN_ROWS = 128
SLOTS = 3

VMEM = pl.BlockSpec(memory_space=pltpu.VMEM)
HBM = pl.BlockSpec(memory_space=pl.ANY)


def column_of(row_vectors, k):
    rows = row_vectors.shape[1]
    first = lax.broadcasted_iota(jnp.int32, (rows, rows), 0)
    second = lax.broadcasted_iota(jnp.int32, (rows, rows), 1)
    spread = jnp.broadcast_to(row_vectors[k : k + 1, :], (rows, rows))
    return jnp.sum(jnp.where(first == second, spread, 0.0), axis=1, keepdims=True)


def norm_kernel(hidden_ref, gain_ref, routes_ref, gates_ref, payload_ref):
    rows, width = hidden_ref.shape
    values = hidden_ref[...].astype(jnp.float32)
    inverse = lax.rsqrt(jnp.mean(values * values, axis=-1, keepdims=True) + EPSILON)
    normed = (values * inverse * gain_ref[...].astype(jnp.float32)).astype(jnp.bfloat16)
    routes = routes_ref[...].astype(jnp.float32)
    gates = gates_ref[...].astype(jnp.float32)
    labels = lax.broadcasted_iota(jnp.int32, (rows, LANES), 1).astype(jnp.float32)
    coefficient = jnp.zeros((rows, LANES), jnp.float32)
    for k in range(routes.shape[0]):
        coefficient += jnp.where(labels == column_of(routes, k), column_of(gates, k), 0.0)
    payload_ref[:, :width] = normed
    payload_ref[:, width:] = coefficient.astype(jnp.bfloat16)


def join_kernel(*refs):
    *pieces, joined = refs
    first = 0
    for piece in pieces:
        rows = piece.shape[0]
        joined[first : first + rows] = piece[...]
        first += rows


def join(pieces, vmem_bytes):
    rows = sum(piece.shape[0] for piece in pieces)
    return pl.pallas_call(
        join_kernel,
        in_specs=[VMEM] * len(pieces),
        out_specs=VMEM,
        out_shape=jax.ShapeDtypeStruct((rows, pieces[0].shape[1]), pieces[0].dtype),
        compiler_params=pltpu.CompilerParams(vmem_limit_bytes=vmem_bytes),
        name="join",
    )(*pieces)


def expert_kernel(
    devices, own_ref, other_ref, gate_ref, w_up_ref, w_down_ref,
    kept_ref, sent_ref, x, hidden, up_slots, down_slots, sems,
):
    half = own_ref.shape[0]
    rows, width = x.shape
    units = hidden.shape[1]
    up_block, down_block = up_slots.shape[2], down_slots.shape[2]
    ups = units // up_block
    downs = width // down_block
    slots = up_slots.shape[0]

    def copy(i):
        if i < ups:
            source = w_up_ref.at[:, pl.ds(i * up_block, up_block)]
            return pltpu.make_async_copy(source, up_slots.at[i % slots], sems.at[i % slots])
        j = i - ups
        source = w_down_ref.at[:, pl.ds(j * down_block, down_block)]
        return pltpu.make_async_copy(source, down_slots.at[j % slots], sems.at[slots + j % slots])

    def start(i):
        if i < ups + downs:
            copy(i).start()

    for i in range(slots):
        start(i)
    x[:half] = own_ref[:, :width]
    x[half : 2 * half] = other_ref[:, :width]
    if rows > 2 * half:
        x[2 * half :] = jnp.zeros((rows - 2 * half, width), x.dtype)

    expert = lax.axis_index(("side", "attn")) // (devices // EXPERTS)
    labels = lax.broadcasted_iota(jnp.int32, (half, LANES), 1)

    def weight_of(ref):
        tail = ref[:, width:].astype(jnp.float32)
        return jnp.sum(jnp.where(labels == expert, tail, 0.0), axis=1, keepdims=True)

    kept_weight, sent_weight = weight_of(own_ref), weight_of(other_ref)

    inputs = x[...]
    for i in range(ups):
        columns = pl.ds(i * up_block, up_block)
        gate = jnp.dot(inputs, gate_ref[:, columns], preferred_element_type=jnp.float32)
        copy(i).wait()
        up = jnp.dot(inputs, up_slots[i % slots], preferred_element_type=jnp.float32)
        start(i + slots)
        hidden[:, columns] = (gate / (1.0 + jnp.exp(-gate)) * up).astype(hidden.dtype)

    activations = hidden[...]

    def finish(weights, first, size):
        out = jnp.dot(activations, weights, preferred_element_type=jnp.float32)
        columns = pl.ds(first, size)
        kept_ref[:, columns] = (out[:half] * kept_weight).astype(kept_ref.dtype)
        sent_ref[:, columns] = (out[half : 2 * half] * sent_weight).astype(sent_ref.dtype)

    for j in range(downs):
        copy(ups + j).wait()
        finish(down_slots[j % slots], j * down_block, down_block)
        start(ups + j + slots)


def divisor(size, wanted):
    return wanted if size % wanted == 0 else size


def swap_sides(values):
    sides = lax.axis_size("side")
    return lax.ppermute(values, "side", [(i, sides - 1 - i) for i in range(sides)])


def swap_chips(values, distance):
    chips = lax.axis_size("attn")
    return lax.ppermute(values, "attn", [(i, i ^ distance) for i in range(chips)])


def shards(hidden_in, norm_gain, routes, route_gates, w_gate, w_up, w_down):
    rows, width = hidden_in.shape
    units = w_gate.shape[1]
    chips = lax.axis_size("attn")
    devices = lax.axis_size("side") * chips
    half = rows * chips
    dtype = jnp.bfloat16
    small = half <= 32
    kernel_bytes = (22 if small else 32) * MIB
    up_block, down_block = divisor(units, 256), 512

    payload = pl.pallas_call(
        norm_kernel,
        in_specs=[VMEM] * 4,
        out_specs=VMEM,
        out_shape=jax.ShapeDtypeStruct((rows, width + LANES), dtype),
        compiler_params=pltpu.CompilerParams(vmem_limit_bytes=4*MIB),
        cost_estimate=pl.CostEstimate(flops=10**11, bytes_accessed=10**6, transcendentals=0),
        name="norm",
    )(hidden_in, norm_gain.reshape(1, width), routes.T, route_gates.T)

    pair = join([payload, swap_chips(payload, 1)], 4*MIB)
    far = [swap_chips(pair, d) for d in range(2, chips, 2)]
    own = join([pair] + far, 4*MIB)
    other = swap_sides(own)

    padded = max(2 * half, MIN_ROWS)
    kept, sent = pl.pallas_call(
        functools.partial(expert_kernel, devices),
        in_specs=[VMEM] * 3 + [HBM] * 2,
        out_specs=[VMEM] * 2,
        out_shape=[jax.ShapeDtypeStruct((half, width), dtype)] * 2,
        scratch_shapes=[
            pltpu.VMEM((padded, width), dtype),
            pltpu.VMEM((padded, units), dtype),
            pltpu.VMEM((SLOTS, width, up_block), dtype),
            pltpu.VMEM((SLOTS, units, down_block), dtype),
            pltpu.SemaphoreType.DMA((2 * SLOTS,)),
        ],
        compiler_params=pltpu.CompilerParams(vmem_limit_bytes=kernel_bytes),
        cost_estimate=pl.CostEstimate(
            flops=12 * half * width * units,
            bytes_accessed=2 * units * 2 * width,
            transcendentals=2 * half * units,
        ),
        name="experts",
    )(
        own,
        other,
        pltpu.with_memory_space_constraint(w_gate, pltpu.VMEM),
        w_up,
        w_down,
    )

    def add(values):
        return sum(v.astype(jnp.float32) for v in values)

    summed = add([kept, swap_sides(sent)]).astype(dtype)
    step = 2 * rows
    arrived = [
        swap_chips(summed[d // 2 * step : (d // 2 + 1) * step], d) for d in range(2, chips, 2)
    ]
    total = add([summed[:step]] + arrived)
    return add([total[:rows], swap_chips(total[rows:].astype(dtype), 1)]).astype(dtype)


def solution(mesh):
    return jax.shard_map(
        shards,
        mesh=mesh,
        in_specs=(
            P(("groups", "side", "attn"), None),
            P(),
            P(("groups", "side", "attn"), None),
            P(("groups", "side", "attn"), None),
            P(None, ("side", "attn")),
            P(None, ("side", "attn")),
            P(("side", "attn"), None),
        ),
        out_specs=P(("groups", "side", "attn"), None),
        check_vma=False,
    )
```

```python
import functools

import jax
import jax.numpy as jnp
from jax import lax
from jax.experimental import pallas as pl
from jax.experimental.pallas import tpu as pltpu
from jax.sharding import PartitionSpec as P

EXPERTS = 4
EPSILON = 1e-05
LANES = 128
MIB = 1 << 20
MIN_ROWS = 128
SLOTS = 2
HELD = 3

VMEM = pl.BlockSpec(memory_space=pltpu.VMEM)
HBM = pl.BlockSpec(memory_space=pl.ANY)


def column_of(row_vectors, k):
    rows = row_vectors.shape[1]
    first = lax.broadcasted_iota(jnp.int32, (rows, rows), 0)
    second = lax.broadcasted_iota(jnp.int32, (rows, rows), 1)
    spread = jnp.broadcast_to(row_vectors[k : k + 1, :], (rows, rows))
    return jnp.sum(jnp.where(first == second, spread, 0.0), axis=1, keepdims=True)


def norm_kernel(*refs):
    sources, payload_ref, buffers, sems = refs[:4], refs[4], refs[5:9], refs[9]
    copies = [
        pltpu.make_async_copy(source, buffer, sems.at[i])
        for i, (source, buffer) in enumerate(zip(sources, buffers))
    ]
    for copy in copies:
        copy.start()
    for copy in copies:
        copy.wait()
    hidden_ref, gain_ref, routes_ref, gates_ref = buffers
    rows, width = hidden_ref.shape
    values = hidden_ref[...].astype(jnp.float32)
    inverse = lax.rsqrt(jnp.mean(values * values, axis=-1, keepdims=True) + EPSILON)
    gain = gain_ref[...].astype(jnp.float32).reshape(1, width)
    normed = (values * inverse * gain).astype(jnp.bfloat16)
    routes = routes_ref[...].astype(jnp.float32)
    gates = gates_ref[...].astype(jnp.float32)
    labels = lax.broadcasted_iota(jnp.int32, (rows, LANES), 1).astype(jnp.float32)
    coefficient = jnp.zeros((rows, LANES), jnp.float32)
    for k in range(routes.shape[0]):
        coefficient += jnp.where(labels == column_of(routes, k), column_of(gates, k), 0.0)
    payload_ref[:, :width] = normed
    payload_ref[:, width:] = coefficient.astype(jnp.bfloat16)


def join_kernel(*refs):
    *pieces, joined = refs
    first = 0
    for piece in pieces:
        rows = piece.shape[0]
        joined[first : first + rows] = piece[...]
        first += rows


def join(pieces, vmem_bytes):
    rows = sum(piece.shape[0] for piece in pieces)
    return pl.pallas_call(
        join_kernel,
        in_specs=[VMEM] * len(pieces),
        out_specs=VMEM,
        out_shape=jax.ShapeDtypeStruct((rows, pieces[0].shape[1]), pieces[0].dtype),
        compiler_params=pltpu.CompilerParams(vmem_limit_bytes=vmem_bytes),
        name="join",
    )(*pieces)


def fetch_kernel(after_ref, w_down_ref, held_ref, sem):
    del after_ref
    columns = held_ref.shape[1]
    copy = pltpu.make_async_copy(w_down_ref.at[:, pl.ds(0, columns)], held_ref, sem)
    copy.start()
    copy.wait()


def expert_kernel(
    devices, even_ref, odd_ref, other_even_ref, other_odd_ref, gate_ref, held_ref, w_up_ref, w_down_ref,
    kept_ref, sent_ref, x, hidden, up_slots, down_slots, sems,
):
    pieces = (even_ref, odd_ref, other_even_ref, other_odd_ref)
    quarter = even_ref.shape[0]
    half = 2 * quarter
    rows, width = x.shape
    units = hidden.shape[1]
    up_block, down_block = up_slots.shape[2], down_slots.shape[2]
    ups = units // up_block
    helds = held_ref.shape[1] // down_block
    downs = width // down_block - helds
    slots = up_slots.shape[0]

    def copy(i):
        if i < ups:
            source = w_up_ref.at[:, pl.ds(i * up_block, up_block)]
            return pltpu.make_async_copy(source, up_slots.at[i % slots], sems.at[i % slots])
        j = i - ups
        source = w_down_ref.at[:, pl.ds((helds + j) * down_block, down_block)]
        return pltpu.make_async_copy(source, down_slots.at[j % slots], sems.at[slots + j % slots])

    def start(i):
        if i < ups + downs:
            copy(i).start()

    for i in range(slots):
        start(i)
    for i, piece in enumerate(pieces):
        x[i * quarter : (i + 1) * quarter] = piece[:, :width]
    if rows > 2 * half:
        x[2 * half :] = jnp.zeros((rows - 2 * half, width), x.dtype)

    expert = lax.axis_index(("side", "attn")) // (devices // EXPERTS)
    labels = lax.broadcasted_iota(jnp.int32, (quarter, LANES), 1)

    def weight_of(ref):
        tail = ref[:, width:].astype(jnp.float32)
        return jnp.sum(jnp.where(labels == expert, tail, 0.0), axis=1, keepdims=True)

    weights = [weight_of(piece) for piece in pieces]

    inputs = x[...]
    for i in range(ups):
        columns = pl.ds(i * up_block, up_block)
        gate = jnp.dot(inputs, gate_ref[:, columns], preferred_element_type=jnp.float32)
        copy(i).wait()
        up = jnp.dot(inputs, up_slots[i % slots], preferred_element_type=jnp.float32)
        start(i + slots)
        hidden[:, columns] = (gate / (1.0 + jnp.exp(-gate)) * up).astype(hidden.dtype)

    activations = hidden[...]

    def finish(block, first):
        out = jnp.dot(activations, block, preferred_element_type=jnp.float32)
        columns = pl.ds(first, down_block)
        for i, weight in enumerate(weights):
            target = (kept_ref, sent_ref)[i // 2]
            piece = out[i * quarter : (i + 1) * quarter] * weight
            target[i % 2 * quarter : (i % 2 + 1) * quarter, columns] = piece.astype(target.dtype)

    for j in range(max(helds, downs)):
        if j < helds:
            finish(held_ref[:, j * down_block : (j + 1) * down_block], j * down_block)
        if j < downs:
            copy(ups + j).wait()
            finish(down_slots[j % slots], (helds + j) * down_block)
            start(ups + j + slots)


def divisor(size, wanted):
    return wanted if size % wanted == 0 else size


def swap_sides(values):
    sides = lax.axis_size("side")
    return lax.ppermute(values, "side", [(i, sides - 1 - i) for i in range(sides)])


def swap_chips(values, distance):
    chips = lax.axis_size("attn")
    return lax.ppermute(values, "attn", [(i, i ^ distance) for i in range(chips)])


def shards(hidden_in, norm_gain, routes, route_gates, w_gate, w_up, w_down):
    rows, width = hidden_in.shape
    units = w_gate.shape[1]
    chips = lax.axis_size("attn")
    devices = lax.axis_size("side") * chips
    half = rows * chips
    dtype = jnp.bfloat16
    w_up = pltpu.with_memory_space_constraint(w_up, pltpu.HBM)
    w_down = pltpu.with_memory_space_constraint(w_down, pltpu.HBM)
    small = half <= 32
    kernel_bytes = (61 if small else 128) * (MIB // 4)
    up_block, down_block = divisor(units, 256), 512
    resident = HELD * down_block

    sources = [hidden_in, norm_gain, routes.T, route_gates.T]
    payload = pl.pallas_call(
        norm_kernel,
        in_specs=[HBM] * 4,
        out_specs=VMEM,
        out_shape=jax.ShapeDtypeStruct((rows, width + LANES), dtype),
        scratch_shapes=[pltpu.VMEM(source.shape, source.dtype) for source in sources]
        + [pltpu.SemaphoreType.DMA((4,))],
        compiler_params=pltpu.CompilerParams(vmem_limit_bytes=4 * MIB),
        cost_estimate=pl.CostEstimate(flops=10**11, bytes_accessed=10**6, transcendentals=0),
        name="norm",
    )(*[pltpu.with_memory_space_constraint(source, pltpu.HBM) for source in sources])

    even = join([payload] + [swap_chips(payload, d) for d in range(2, chips, 2)], 4 * MIB)
    odd = swap_chips(even, 1)
    other_even = swap_sides(even)
    held = pl.pallas_call(
        fetch_kernel,
        in_specs=[HBM] * 2,
        out_specs=VMEM,
        out_shape=pltpu.VMEM((units, resident), dtype),
        scratch_shapes=[pltpu.SemaphoreType.DMA],
        compiler_params=pltpu.CompilerParams(vmem_limit_bytes=4 * MIB),
        cost_estimate=pl.CostEstimate(
            flops=0, bytes_accessed=2 * units * resident, transcendentals=0
        ),
        name="fetch",
    )(even, w_down)
    odd, held = lax.optimization_barrier((odd, held))
    other_odd = swap_sides(odd)

    padded = max(2 * half, MIN_ROWS)
    kept, sent = pl.pallas_call(
        functools.partial(expert_kernel, devices),
        in_specs=[VMEM] * 6 + [HBM] * 2,
        out_specs=[VMEM] * 2,
        out_shape=[jax.ShapeDtypeStruct((half, width), dtype)] * 2,
        scratch_shapes=[
            pltpu.VMEM((padded, width), dtype),
            pltpu.VMEM((padded, units), dtype),
            pltpu.VMEM((SLOTS, width, up_block), dtype),
            pltpu.VMEM((SLOTS, units, down_block), dtype),
            pltpu.SemaphoreType.DMA((2 * SLOTS,)),
        ],
        compiler_params=pltpu.CompilerParams(vmem_limit_bytes=kernel_bytes),
        cost_estimate=pl.CostEstimate(
            flops=12 * half * width * units,
            bytes_accessed=2 * units * (2 * width - resident),
            transcendentals=2 * half * units,
        ),
        name="experts",
    )(
        even,
        odd,
        other_even,
        other_odd,
        pltpu.with_memory_space_constraint(w_gate, pltpu.VMEM),
        pltpu.with_memory_space_constraint(held, pltpu.VMEM),
        w_up,
        w_down,
    )

    def add(values):
        return sum(v.astype(jnp.float32) for v in values)

    summed = add([kept, swap_sides(sent)]).astype(dtype)
    middle = half // 2
    plane = add([summed[:middle], swap_chips(summed[middle:], 1)]).astype(dtype)
    arrived = [
        swap_chips(plane[d // 2 * rows : (d // 2 + 1) * rows], d) for d in range(2, chips, 2)
    ]
    return add([plane[:rows]] + arrived).astype(dtype)


def solution(mesh):
    return jax.shard_map(
        shards,
        mesh=mesh,
        in_specs=(
            P(("groups", "side", "attn"), None),
            P(),
            P(("groups", "side", "attn"), None),
            P(("groups", "side", "attn"), None),
            P(None, ("side", "attn")),
            P(None, ("side", "attn")),
            P(("side", "attn"), None),
        ),
        out_specs=P(("groups", "side", "attn"), None),
        check_vma=False,
    )
```

```python
import functools

import jax
import jax.numpy as jnp
from jax import lax
from jax.experimental import pallas as pl
from jax.experimental.pallas import tpu as pltpu
from jax.sharding import PartitionSpec as P

EXPERTS = 4
EPSILON = 1e-05
LANES = 128
MIB = 1 << 20
MIN_ROWS = 128
SLOTS = 4
HELD = 2

VMEM = pl.BlockSpec(memory_space=pltpu.VMEM)
HBM = pl.BlockSpec(memory_space=pl.ANY)


def column_of(row_vectors, k):
    rows = row_vectors.shape[1]
    first = lax.broadcasted_iota(jnp.int32, (rows, rows), 0)
    second = lax.broadcasted_iota(jnp.int32, (rows, rows), 1)
    spread = jnp.broadcast_to(row_vectors[k : k + 1, :], (rows, rows))
    return jnp.sum(jnp.where(first == second, spread, 0.0), axis=1, keepdims=True)


def norm_kernel(*refs):
    sources, payload_ref, buffers, sems = refs[:4], refs[4], refs[5:9], refs[9]
    copies = [
        pltpu.make_async_copy(source, buffer, sems.at[i])
        for i, (source, buffer) in enumerate(zip(sources, buffers))
    ]
    for copy in copies:
        copy.start()
    for copy in copies:
        copy.wait()
    hidden_ref, gain_ref, routes_ref, gates_ref = buffers
    rows, width = hidden_ref.shape
    values = hidden_ref[...].astype(jnp.float32)
    inverse = lax.rsqrt(jnp.mean(values * values, axis=-1, keepdims=True) + EPSILON)
    gain = gain_ref[...].astype(jnp.float32).reshape(1, width)
    normed = (values * inverse * gain).astype(jnp.bfloat16)
    routes = routes_ref[...].astype(jnp.float32)
    gates = gates_ref[...].astype(jnp.float32)
    labels = lax.broadcasted_iota(jnp.int32, (rows, LANES), 1).astype(jnp.float32)
    coefficient = jnp.zeros((rows, LANES), jnp.float32)
    for k in range(routes.shape[0]):
        coefficient += jnp.where(labels == column_of(routes, k), column_of(gates, k), 0.0)
    payload_ref[:, :width] = normed
    payload_ref[:, width:] = coefficient.astype(jnp.bfloat16)


def join_kernel(*refs):
    *pieces, joined = refs
    first = 0
    for piece in pieces:
        rows = piece.shape[0]
        joined[first : first + rows] = piece[...]
        first += rows


def join(pieces, vmem_bytes):
    rows = sum(piece.shape[0] for piece in pieces)
    return pl.pallas_call(
        join_kernel,
        in_specs=[VMEM] * len(pieces),
        out_specs=VMEM,
        out_shape=jax.ShapeDtypeStruct((rows, pieces[0].shape[1]), pieces[0].dtype),
        compiler_params=pltpu.CompilerParams(vmem_limit_bytes=vmem_bytes),
        name="join",
    )(*pieces)


def fetch_kernel(after_ref, w_down_ref, held_ref, sem):
    del after_ref
    columns = held_ref.shape[1]
    copy = pltpu.make_async_copy(w_down_ref.at[:, pl.ds(0, columns)], held_ref, sem)
    copy.start()
    copy.wait()


def expert_kernel(
    devices, up_block, down_block, even_ref, odd_ref, other_even_ref, other_odd_ref, gate_ref, held_ref,
    w_up_ref, w_down_ref, kept_ref, sent_ref, x, hidden, slots, sems,
):
    pieces = (even_ref, odd_ref, other_even_ref, other_odd_ref)
    quarter = even_ref.shape[0]
    half = 2 * quarter
    rows, width = x.shape
    units = hidden.shape[1]
    count = slots.shape[0]
    depth = width // 2
    ups = 2 * units // up_block
    helds = held_ref.shape[1] // down_block
    downs = width // down_block - helds

    def slot(i):
        if i < ups:
            return slots.at[i % count, pl.ds(0, depth), pl.ds(0, up_block)]
        return slots.at[i % count, pl.ds(0, units), pl.ds(0, down_block)]

    def copy(i):
        if i < ups:
            lanes = pl.ds(i // 2 * up_block, up_block)
            source = w_up_ref.at[pl.ds(i % 2 * depth, depth), lanes]
        else:
            source = w_down_ref.at[:, pl.ds((helds + i - ups) * down_block, down_block)]
        return pltpu.make_async_copy(source, slot(i), sems.at[i % count])

    def start(i):
        if i < ups + downs:
            copy(i).start()

    for i in range(count):
        start(i)
    for i, piece in enumerate(pieces):
        x[i * quarter : (i + 1) * quarter] = piece[:, :width]
    if rows > 2 * half:
        x[2 * half :] = jnp.zeros((rows - 2 * half, width), x.dtype)

    expert = lax.axis_index(("side", "attn")) // (devices // EXPERTS)
    labels = lax.broadcasted_iota(jnp.int32, (quarter, LANES), 1)

    def weight_of(ref):
        tail = ref[:, width:].astype(jnp.float32)
        return jnp.sum(jnp.where(labels == expert, tail, 0.0), axis=1, keepdims=True)

    weights = [weight_of(piece) for piece in pieces]

    inputs = x[...]
    for i in range(ups // 2):
        columns = pl.ds(i * up_block, up_block)
        gate = jnp.dot(inputs, gate_ref[:, columns], preferred_element_type=jnp.float32)
        terms = []
        for k in range(2):
            copy(2 * i + k).wait()
            part = inputs[:, k * depth : (k + 1) * depth]
            terms.append(jnp.dot(part, slot(2 * i + k)[...], preferred_element_type=jnp.float32))
            start(2 * i + k + count)
        up = terms[0] + terms[1]
        hidden[:, columns] = (gate / (1.0 + jnp.exp(-gate)) * up).astype(hidden.dtype)

    activations = hidden[...]

    def finish(block, first):
        out = jnp.dot(activations, block, preferred_element_type=jnp.float32)
        columns = pl.ds(first, down_block)
        for i, weight in enumerate(weights):
            target = (kept_ref, sent_ref)[i // 2]
            piece = out[i * quarter : (i + 1) * quarter] * weight
            target[i % 2 * quarter : (i % 2 + 1) * quarter, columns] = piece.astype(target.dtype)

    for j in range(max(helds, downs)):
        if j < helds:
            finish(held_ref[:, j * down_block : (j + 1) * down_block], j * down_block)
        if j < downs:
            copy(ups + j).wait()
            finish(slot(ups + j)[...], (helds + j) * down_block)
            start(ups + j + count)


def divisor(size, wanted):
    return wanted if size % wanted == 0 else size


def swap_sides(values):
    sides = lax.axis_size("side")
    return lax.ppermute(values, "side", [(i, sides - 1 - i) for i in range(sides)])


def swap_chips(values, distance):
    chips = lax.axis_size("attn")
    return lax.ppermute(values, "attn", [(i, i ^ distance) for i in range(chips)])


def shards(hidden_in, norm_gain, routes, route_gates, w_gate, w_up, w_down):
    rows, width = hidden_in.shape
    units = w_gate.shape[1]
    chips = lax.axis_size("attn")
    devices = lax.axis_size("side") * chips
    half = rows * chips
    dtype = jnp.bfloat16
    w_up = pltpu.with_memory_space_constraint(w_up, pltpu.HBM)
    w_down = pltpu.with_memory_space_constraint(w_down, pltpu.HBM)
    small = half <= 32
    kernel_bytes = (68 if small else 128) * (MIB // 4)
    up_block, down_block = divisor(units, 512), 512 if units % 512 == 0 else 256
    resident = HELD * down_block

    sources = [hidden_in, norm_gain, routes.T, route_gates.T]
    payload = pl.pallas_call(
        norm_kernel,
        in_specs=[HBM] * 4,
        out_specs=VMEM,
        out_shape=jax.ShapeDtypeStruct((rows, width + LANES), dtype),
        scratch_shapes=[pltpu.VMEM(source.shape, source.dtype) for source in sources]
        + [pltpu.SemaphoreType.DMA((4,))],
        compiler_params=pltpu.CompilerParams(vmem_limit_bytes=4 * MIB),
        cost_estimate=pl.CostEstimate(flops=10**11, bytes_accessed=10**6, transcendentals=0),
        name="norm",
    )(*[pltpu.with_memory_space_constraint(source, pltpu.HBM) for source in sources])

    even = join([payload] + [swap_chips(payload, d) for d in range(2, chips, 2)], 4 * MIB)
    odd = swap_chips(even, 1)
    other_even = swap_sides(even)
    held = pl.pallas_call(
        fetch_kernel,
        in_specs=[HBM] * 2,
        out_specs=VMEM,
        out_shape=pltpu.VMEM((units, resident), dtype),
        scratch_shapes=[pltpu.SemaphoreType.DMA],
        compiler_params=pltpu.CompilerParams(vmem_limit_bytes=4 * MIB),
        cost_estimate=pl.CostEstimate(
            flops=0, bytes_accessed=2 * units * resident, transcendentals=0
        ),
        name="fetch",
    )(even, w_down)
    odd, held = lax.optimization_barrier((odd, held))
    other_odd = swap_sides(odd)

    padded = max(2 * half, MIN_ROWS)
    kept, sent = pl.pallas_call(
        functools.partial(expert_kernel, devices, up_block, down_block),
        in_specs=[VMEM] * 6 + [HBM] * 2,
        out_specs=[VMEM] * 2,
        out_shape=[jax.ShapeDtypeStruct((half, width), dtype)] * 2,
        scratch_shapes=[
            pltpu.VMEM((padded, width), dtype),
            pltpu.VMEM((padded, units), dtype),
            pltpu.VMEM((SLOTS, max(width // 2, units), max(up_block, down_block)), dtype),
            pltpu.SemaphoreType.DMA((SLOTS,)),
        ],
        compiler_params=pltpu.CompilerParams(vmem_limit_bytes=kernel_bytes),
        cost_estimate=pl.CostEstimate(
            flops=12 * half * width * units,
            bytes_accessed=2 * units * (2 * width - resident),
            transcendentals=2 * half * units,
        ),
        name="experts",
    )(
        even,
        odd,
        other_even,
        other_odd,
        pltpu.with_memory_space_constraint(w_gate, pltpu.VMEM),
        pltpu.with_memory_space_constraint(held, pltpu.VMEM),
        w_up,
        w_down,
    )

    def add(values):
        return sum(v.astype(jnp.float32) for v in values)

    summed = add([kept, swap_sides(sent)]).astype(dtype)
    middle = half // 2
    plane = add([summed[:middle], swap_chips(summed[middle:], 1)]).astype(dtype)
    arrived = [
        swap_chips(plane[d // 2 * rows : (d // 2 + 1) * rows], d) for d in range(2, chips, 2)
    ]
    return add([plane[:rows]] + arrived).astype(dtype)


def solution(mesh):
    return jax.shard_map(
        shards,
        mesh=mesh,
        in_specs=(
            P(("groups", "side", "attn"), None),
            P(),
            P(("groups", "side", "attn"), None),
            P(("groups", "side", "attn"), None),
            P(None, ("side", "attn")),
            P(None, ("side", "attn")),
            P(("side", "attn"), None),
        ),
        out_specs=P(("groups", "side", "attn"), None),
        check_vma=False,
    )
```

```python
import functools

import jax
import jax.numpy as jnp
from jax import lax
from jax.experimental import pallas as pl
from jax.experimental.pallas import tpu as pltpu
from jax.sharding import PartitionSpec as P

EXPERTS = 4
EPSILON = 1e-05
LANES = 128
MIB = 1 << 20
MIN_ROWS = 128
SLOTS = 4
HELD = 2

VMEM = pl.BlockSpec(memory_space=pltpu.VMEM)
HBM = pl.BlockSpec(memory_space=pl.ANY)


def column_of(row_vectors, k):
    rows = row_vectors.shape[1]
    first = lax.broadcasted_iota(jnp.int32, (rows, rows), 0)
    second = lax.broadcasted_iota(jnp.int32, (rows, rows), 1)
    spread = jnp.broadcast_to(row_vectors[k : k + 1, :], (rows, rows))
    return jnp.sum(jnp.where(first == second, spread, 0.0), axis=1, keepdims=True)


def norm_kernel(*refs):
    sources, payload_ref, buffers, sems = refs[:4], refs[4], refs[5:9], refs[9]
    copies = [
        pltpu.make_async_copy(source, buffer, sems.at[i])
        for i, (source, buffer) in enumerate(zip(sources, buffers))
    ]
    for copy in copies:
        copy.start()
    for copy in copies:
        copy.wait()
    hidden_ref, gain_ref, routes_ref, gates_ref = buffers
    rows, width = hidden_ref.shape
    values = hidden_ref[...].astype(jnp.float32)
    inverse = lax.rsqrt(jnp.mean(values * values, axis=-1, keepdims=True) + EPSILON)
    gain = gain_ref[...].astype(jnp.float32).reshape(1, width)
    normed = (values * inverse * gain).astype(jnp.bfloat16)
    routes = routes_ref[...].astype(jnp.float32)
    gates = gates_ref[...].astype(jnp.float32)
    labels = lax.broadcasted_iota(jnp.int32, (rows, LANES), 1).astype(jnp.float32)
    coefficient = jnp.zeros((rows, LANES), jnp.float32)
    for k in range(routes.shape[0]):
        coefficient += jnp.where(labels == column_of(routes, k), column_of(gates, k), 0.0)
    payload_ref[:, :width] = normed
    payload_ref[:, width:] = coefficient.astype(jnp.bfloat16)


def join_kernel(*refs):
    *pieces, joined = refs
    first = 0
    for piece in pieces:
        rows = piece.shape[0]
        joined[first : first + rows] = piece[...]
        first += rows


def join(pieces, vmem_bytes):
    rows = sum(piece.shape[0] for piece in pieces)
    return pl.pallas_call(
        join_kernel,
        in_specs=[VMEM] * len(pieces),
        out_specs=VMEM,
        out_shape=jax.ShapeDtypeStruct((rows, pieces[0].shape[1]), pieces[0].dtype),
        compiler_params=pltpu.CompilerParams(vmem_limit_bytes=vmem_bytes),
        name="join",
    )(*pieces)


def fetch_kernel(after_ref, w_down_ref, held_ref, sem):
    del after_ref
    columns = held_ref.shape[1]
    copy = pltpu.make_async_copy(w_down_ref.at[:, pl.ds(0, columns)], held_ref, sem)
    copy.start()
    copy.wait()


def expert_kernel(
    devices, up_block, down_block, even_ref, odd_ref, other_even_ref, other_odd_ref, gate_ref, held_ref,
    w_up_ref, w_down_ref, kept_even_ref, kept_odd_ref, sent_even_ref, sent_odd_ref, x, hidden, slots, sems,
):
    pieces = (even_ref, odd_ref, other_even_ref, other_odd_ref)
    quarter = even_ref.shape[0]
    half = 2 * quarter
    rows, width = x.shape
    units = hidden.shape[1]
    count = slots.shape[0]
    depth = width // 2
    ups = 2 * units // up_block
    helds = held_ref.shape[1] // down_block
    downs = width // down_block - helds

    def slot(i):
        if i < ups:
            return slots.at[i % count, pl.ds(0, depth), pl.ds(0, up_block)]
        return slots.at[i % count, pl.ds(0, units), pl.ds(0, down_block)]

    def copy(i):
        if i < ups:
            lanes = pl.ds(i // 2 * up_block, up_block)
            source = w_up_ref.at[pl.ds(i % 2 * depth, depth), lanes]
        else:
            source = w_down_ref.at[:, pl.ds((helds + i - ups) * down_block, down_block)]
        return pltpu.make_async_copy(source, slot(i), sems.at[i % count])

    def start(i):
        if i < ups + downs:
            copy(i).start()

    for i in range(count):
        start(i)
    for i, piece in enumerate(pieces):
        x[i * quarter : (i + 1) * quarter] = piece[:, :width]
    if rows > 2 * half:
        x[2 * half :] = jnp.zeros((rows - 2 * half, width), x.dtype)

    expert = lax.axis_index(("side", "attn")) // (devices // EXPERTS)
    labels = lax.broadcasted_iota(jnp.int32, (quarter, LANES), 1)

    def weight_of(ref):
        tail = ref[:, width:].astype(jnp.float32)
        return jnp.sum(jnp.where(labels == expert, tail, 0.0), axis=1, keepdims=True)

    weights = [weight_of(piece) for piece in pieces]

    inputs = x[...]
    for i in range(ups // 2):
        columns = pl.ds(i * up_block, up_block)
        gate = jnp.dot(inputs, gate_ref[:, columns], preferred_element_type=jnp.float32)
        terms = []
        for k in range(2):
            copy(2 * i + k).wait()
            part = inputs[:, k * depth : (k + 1) * depth]
            terms.append(jnp.dot(part, slot(2 * i + k)[...], preferred_element_type=jnp.float32))
            start(2 * i + k + count)
        up = terms[0] + terms[1]
        hidden[:, columns] = (gate / (1.0 + jnp.exp(-gate)) * up).astype(hidden.dtype)

    activations = hidden[...]
    targets = (kept_even_ref, kept_odd_ref, sent_even_ref, sent_odd_ref)

    def finish(block, first):
        out = jnp.dot(activations, block, preferred_element_type=jnp.float32)
        columns = pl.ds(first, down_block)
        for i, (weight, target) in enumerate(zip(weights, targets)):
            piece = out[i * quarter : (i + 1) * quarter] * weight
            target[:, columns] = piece.astype(target.dtype)

    for j in range(max(helds, downs)):
        if j < helds:
            finish(held_ref[:, j * down_block : (j + 1) * down_block], j * down_block)
        if j < downs:
            copy(ups + j).wait()
            finish(slot(ups + j)[...], (helds + j) * down_block)
            start(ups + j + count)


def divisor(size, wanted):
    return wanted if size % wanted == 0 else size


def swap_sides(values):
    sides = lax.axis_size("side")
    return lax.ppermute(values, "side", [(i, sides - 1 - i) for i in range(sides)])


def swap_chips(values, distance):
    chips = lax.axis_size("attn")
    return lax.ppermute(values, "attn", [(i, i ^ distance) for i in range(chips)])


def shards(hidden_in, norm_gain, routes, route_gates, w_gate, w_up, w_down):
    rows, width = hidden_in.shape
    units = w_gate.shape[1]
    chips = lax.axis_size("attn")
    devices = lax.axis_size("side") * chips
    half = rows * chips
    dtype = jnp.bfloat16
    w_up = pltpu.with_memory_space_constraint(w_up, pltpu.HBM)
    w_down = pltpu.with_memory_space_constraint(w_down, pltpu.HBM)
    small = half <= 32
    kernel_bytes = (68 if small else 128) * (MIB // 4)
    up_block, down_block = divisor(units, 512), 512 if units % 512 == 0 else 256
    resident = HELD * down_block

    sources = [hidden_in, norm_gain, routes.T, route_gates.T]
    payload = pl.pallas_call(
        norm_kernel,
        in_specs=[HBM] * 4,
        out_specs=VMEM,
        out_shape=jax.ShapeDtypeStruct((rows, width + LANES), dtype),
        scratch_shapes=[pltpu.VMEM(source.shape, source.dtype) for source in sources]
        + [pltpu.SemaphoreType.DMA((4,))],
        compiler_params=pltpu.CompilerParams(vmem_limit_bytes=4 * MIB),
        cost_estimate=pl.CostEstimate(flops=10**11, bytes_accessed=10**6, transcendentals=0),
        name="norm",
    )(*[pltpu.with_memory_space_constraint(source, pltpu.HBM) for source in sources])

    even = join([payload] + [swap_chips(payload, d) for d in range(2, chips, 2)], 4 * MIB)
    odd = swap_chips(even, 1)
    other_even = swap_sides(even)
    held = pl.pallas_call(
        fetch_kernel,
        in_specs=[HBM] * 2,
        out_specs=VMEM,
        out_shape=pltpu.VMEM((units, resident), dtype),
        scratch_shapes=[pltpu.SemaphoreType.DMA],
        compiler_params=pltpu.CompilerParams(vmem_limit_bytes=4 * MIB),
        cost_estimate=pl.CostEstimate(
            flops=0, bytes_accessed=2 * units * resident, transcendentals=0
        ),
        name="fetch",
    )(even, w_down)
    odd, held = lax.optimization_barrier((odd, held))
    other_odd = swap_sides(odd)

    padded = max(2 * half, MIN_ROWS)
    kept_even, kept_odd, sent_even, sent_odd = pl.pallas_call(
        functools.partial(expert_kernel, devices, up_block, down_block),
        in_specs=[VMEM] * 6 + [HBM] * 2,
        out_specs=[VMEM] * 4,
        out_shape=[jax.ShapeDtypeStruct((half // 2, width), dtype)] * 4,
        scratch_shapes=[
            pltpu.VMEM((padded, width), dtype),
            pltpu.VMEM((padded, units), dtype),
            pltpu.VMEM((SLOTS, max(width // 2, units), max(up_block, down_block)), dtype),
            pltpu.SemaphoreType.DMA((SLOTS,)),
        ],
        compiler_params=pltpu.CompilerParams(vmem_limit_bytes=kernel_bytes),
        cost_estimate=pl.CostEstimate(
            flops=12 * half * width * units,
            bytes_accessed=2 * units * (2 * width - resident),
            transcendentals=2 * half * units,
        ),
        name="experts",
    )(
        even,
        odd,
        other_even,
        other_odd,
        pltpu.with_memory_space_constraint(w_gate, pltpu.VMEM),
        pltpu.with_memory_space_constraint(held, pltpu.VMEM),
        w_up,
        w_down,
    )

    def add(values):
        return sum(v.astype(jnp.float32) for v in values)

    odd_sum = add([kept_odd, swap_sides(sent_odd)]).astype(dtype)
    plane = add([kept_even, swap_sides(sent_even), swap_chips(odd_sum, 1)]).astype(dtype)
    arrived = [
        swap_chips(plane[d // 2 * rows : (d // 2 + 1) * rows], d) for d in range(2, chips, 2)
    ]
    return add([plane[:rows]] + arrived).astype(dtype)


def solution(mesh):
    return jax.shard_map(
        shards,
        mesh=mesh,
        in_specs=(
            P(("groups", "side", "attn"), None),
            P(),
            P(("groups", "side", "attn"), None),
            P(("groups", "side", "attn"), None),
            P(None, ("side", "attn")),
            P(None, ("side", "attn")),
            P(("side", "attn"), None),
        ),
        out_specs=P(("groups", "side", "attn"), None),
        check_vma=False,
    )
```

```python
import functools

import jax
import jax.numpy as jnp
from jax import lax
from jax.experimental import pallas as pl
from jax.experimental.pallas import tpu as pltpu
from jax.sharding import PartitionSpec as P

EXPERTS = 4
EPSILON = 1e-05
LANES = 128
MIB = 1 << 20
MIN_ROWS = 128
SLOTS = 4
HELD = 2

VMEM = pl.BlockSpec(memory_space=pltpu.VMEM)
HBM = pl.BlockSpec(memory_space=pl.ANY)


def column_of(row_vectors, k):
    rows = row_vectors.shape[1]
    first = lax.broadcasted_iota(jnp.int32, (rows, rows), 0)
    second = lax.broadcasted_iota(jnp.int32, (rows, rows), 1)
    spread = jnp.broadcast_to(row_vectors[k : k + 1, :], (rows, rows))
    return jnp.sum(jnp.where(first == second, spread, 0.0), axis=1, keepdims=True)


def norm_kernel(*refs):
    sources, payload_ref, buffers, sems = refs[:4], refs[4], refs[5:9], refs[9]
    copies = [
        pltpu.make_async_copy(source, buffer, sems.at[i])
        for i, (source, buffer) in enumerate(zip(sources, buffers))
    ]
    for copy in copies:
        copy.start()
    for copy in copies:
        copy.wait()
    hidden_ref, gain_ref, routes_ref, gates_ref = buffers
    rows, width = hidden_ref.shape
    values = hidden_ref[...].astype(jnp.float32)
    inverse = lax.rsqrt(jnp.mean(values * values, axis=-1, keepdims=True) + EPSILON)
    gain = gain_ref[...].astype(jnp.float32).reshape(1, width)
    normed = (values * inverse * gain).astype(jnp.bfloat16)
    routes = routes_ref[...].astype(jnp.float32)
    gates = gates_ref[...].astype(jnp.float32)
    labels = lax.broadcasted_iota(jnp.int32, (rows, LANES), 1).astype(jnp.float32)
    coefficient = jnp.zeros((rows, LANES), jnp.float32)
    for k in range(routes.shape[0]):
        coefficient += jnp.where(labels == column_of(routes, k), column_of(gates, k), 0.0)
    payload_ref[:, :width] = normed
    payload_ref[:, width:] = coefficient.astype(jnp.bfloat16)


def join_kernel(*refs):
    *pieces, joined = refs
    first = 0
    for piece in pieces:
        rows = piece.shape[0]
        joined[first : first + rows] = piece[...]
        first += rows


def join(pieces, vmem_bytes):
    rows = sum(piece.shape[0] for piece in pieces)
    return pl.pallas_call(
        join_kernel,
        in_specs=[VMEM] * len(pieces),
        out_specs=VMEM,
        out_shape=jax.ShapeDtypeStruct((rows, pieces[0].shape[1]), pieces[0].dtype),
        compiler_params=pltpu.CompilerParams(vmem_limit_bytes=vmem_bytes),
        name="join",
    )(*pieces)


def fetch_kernel(after_ref, w_down_ref, held_ref, sem):
    del after_ref
    columns = held_ref.shape[1]
    copy = pltpu.make_async_copy(w_down_ref.at[:, pl.ds(0, columns)], held_ref, sem)
    copy.start()
    copy.wait()


def expert_kernel(
    devices, up_block, down_block, even_ref, odd_ref, other_even_ref, other_odd_ref, gate_ref, held_ref,
    w_up_ref, w_down_ref, kept_even_ref, kept_odd_ref, sent_even_ref, sent_odd_ref, x, hidden, slots, sems,
):
    pieces = (even_ref, odd_ref, other_even_ref, other_odd_ref)
    quarter = even_ref.shape[0]
    half = 2 * quarter
    rows, width = x.shape
    units = hidden.shape[1]
    count = slots.shape[0]
    depth = width // 2
    ups = 2 * units // up_block
    helds = held_ref.shape[1] // down_block
    downs = width // down_block - helds

    def slot(i):
        if i < ups:
            return slots.at[i % count, pl.ds(0, depth), pl.ds(0, up_block)]
        return slots.at[i % count, pl.ds(0, units), pl.ds(0, down_block)]

    def copy(i):
        if i < ups:
            lanes = pl.ds(i // 2 * up_block, up_block)
            source = w_up_ref.at[pl.ds(i % 2 * depth, depth), lanes]
        else:
            source = w_down_ref.at[:, pl.ds((helds + i - ups) * down_block, down_block)]
        return pltpu.make_async_copy(source, slot(i), sems.at[i % count])

    def start(i):
        if i < ups + downs:
            copy(i).start()

    for i in range(count):
        start(i)
    for i, piece in enumerate(pieces):
        x[i * quarter : (i + 1) * quarter] = piece[:, :width]
    if rows > 2 * half:
        x[2 * half :] = jnp.zeros((rows - 2 * half, width), x.dtype)

    expert = lax.axis_index(("side", "attn")) // (devices // EXPERTS)
    labels = lax.broadcasted_iota(jnp.int32, (quarter, LANES), 1)

    def weight_of(ref):
        tail = ref[:, width:].astype(jnp.float32)
        return jnp.sum(jnp.where(labels == expert, tail, 0.0), axis=1, keepdims=True)

    weights = [weight_of(piece) for piece in pieces]

    inputs = x[...]
    for i in range(ups // 2):
        columns = pl.ds(i * up_block, up_block)
        gate = jnp.dot(inputs, gate_ref[:, columns], preferred_element_type=jnp.float32)
        terms = []
        for k in range(2):
            copy(2 * i + k).wait()
            part = inputs[:, k * depth : (k + 1) * depth]
            terms.append(jnp.dot(part, slot(2 * i + k)[...], preferred_element_type=jnp.float32))
            start(2 * i + k + count)
        up = terms[0] + terms[1]
        hidden[:, columns] = (gate / (1.0 + jnp.exp(-gate)) * up).astype(hidden.dtype)

    activations = hidden[...]
    targets = (kept_even_ref, kept_odd_ref, sent_even_ref, sent_odd_ref)

    def finish(block, first):
        out = jnp.dot(activations, block, preferred_element_type=jnp.float32)
        columns = pl.ds(first, down_block)
        for i, (weight, target) in enumerate(zip(weights, targets)):
            piece = out[i * quarter : (i + 1) * quarter] * weight
            target[:, columns] = piece.astype(target.dtype)

    late = max(downs - helds, 0)
    for j in range(max(late + helds, downs)):
        if j >= late:
            first = (j - late) * down_block
            finish(held_ref[:, first : first + down_block], first)
        if j < downs:
            copy(ups + j).wait()
            finish(slot(ups + j)[...], (helds + j) * down_block)
            start(ups + j + count)


def divisor(size, wanted):
    return wanted if size % wanted == 0 else size


def swap_sides(values):
    sides = lax.axis_size("side")
    return lax.ppermute(values, "side", [(i, sides - 1 - i) for i in range(sides)])


def swap_chips(values, distance):
    chips = lax.axis_size("attn")
    return lax.ppermute(values, "attn", [(i, i ^ distance) for i in range(chips)])


def shards(hidden_in, norm_gain, routes, route_gates, w_gate, w_up, w_down):
    rows, width = hidden_in.shape
    units = w_gate.shape[1]
    chips = lax.axis_size("attn")
    devices = lax.axis_size("side") * chips
    half = rows * chips
    dtype = jnp.bfloat16
    w_up = pltpu.with_memory_space_constraint(w_up, pltpu.HBM)
    w_down = pltpu.with_memory_space_constraint(w_down, pltpu.HBM)
    small = half <= 32
    kernel_bytes = (68 if small else 128) * (MIB // 4)
    up_block, down_block = divisor(units, 512), 512 if units % 512 == 0 else 256
    resident = HELD * down_block

    sources = [hidden_in, norm_gain, routes.T, route_gates.T]
    payload = pl.pallas_call(
        norm_kernel,
        in_specs=[HBM] * 4,
        out_specs=VMEM,
        out_shape=jax.ShapeDtypeStruct((rows, width + LANES), dtype),
        scratch_shapes=[pltpu.VMEM(source.shape, source.dtype) for source in sources]
        + [pltpu.SemaphoreType.DMA((4,))],
        compiler_params=pltpu.CompilerParams(vmem_limit_bytes=4 * MIB),
        cost_estimate=pl.CostEstimate(flops=10**11, bytes_accessed=10**6, transcendentals=0),
        name="norm",
    )(*[pltpu.with_memory_space_constraint(source, pltpu.HBM) for source in sources])

    even = join([payload] + [swap_chips(payload, d) for d in range(2, chips, 2)], 4 * MIB)
    odd = swap_chips(even, 1)
    other_even = swap_sides(even)
    held = pl.pallas_call(
        fetch_kernel,
        in_specs=[HBM] * 2,
        out_specs=VMEM,
        out_shape=pltpu.VMEM((units, resident), dtype),
        scratch_shapes=[pltpu.SemaphoreType.DMA],
        compiler_params=pltpu.CompilerParams(vmem_limit_bytes=4 * MIB),
        cost_estimate=pl.CostEstimate(
            flops=0, bytes_accessed=2 * units * resident, transcendentals=0
        ),
        name="fetch",
    )(even, w_down)
    odd, held = lax.optimization_barrier((odd, held))
    other_odd = swap_sides(odd)

    padded = max(2 * half, MIN_ROWS)
    kept_even, kept_odd, sent_even, sent_odd = pl.pallas_call(
        functools.partial(expert_kernel, devices, up_block, down_block),
        in_specs=[VMEM] * 6 + [HBM] * 2,
        out_specs=[VMEM] * 4,
        out_shape=[jax.ShapeDtypeStruct((half // 2, width), dtype)] * 4,
        scratch_shapes=[
            pltpu.VMEM((padded, width), dtype),
            pltpu.VMEM((padded, units), dtype),
            pltpu.VMEM((SLOTS, max(width // 2, units), max(up_block, down_block)), dtype),
            pltpu.SemaphoreType.DMA((SLOTS,)),
        ],
        compiler_params=pltpu.CompilerParams(vmem_limit_bytes=kernel_bytes),
        cost_estimate=pl.CostEstimate(
            flops=12 * half * width * units,
            bytes_accessed=2 * units * (2 * width - resident),
            transcendentals=2 * half * units,
        ),
        name="experts",
    )(
        even,
        odd,
        other_even,
        other_odd,
        pltpu.with_memory_space_constraint(w_gate, pltpu.VMEM),
        pltpu.with_memory_space_constraint(held, pltpu.VMEM),
        w_up,
        w_down,
    )

    def add(values):
        return sum(v.astype(jnp.float32) for v in values)

    odd_sum = add([kept_odd, swap_sides(sent_odd)]).astype(dtype)
    plane = add([kept_even, swap_sides(sent_even), swap_chips(odd_sum, 1)]).astype(dtype)
    arrived = [
        swap_chips(plane[d // 2 * rows : (d // 2 + 1) * rows], d) for d in range(2, chips, 2)
    ]
    return add([plane[:rows]] + arrived).astype(dtype)


def solution(mesh):
    return jax.shard_map(
        shards,
        mesh=mesh,
        in_specs=(
            P(("groups", "side", "attn"), None),
            P(),
            P(("groups", "side", "attn"), None),
            P(("groups", "side", "attn"), None),
            P(None, ("side", "attn")),
            P(None, ("side", "attn")),
            P(("side", "attn"), None),
        ),
        out_specs=P(("groups", "side", "attn"), None),
        check_vma=False,
    )
```
